512 devices in a mesh: expert: 32 (over z, core), hidden: 16 (over x, y).
Axes of the slice: x: 4, y: 4, z: 16, core: 2. Of those that a mesh axis runs over, the one named last changes fastest.
Arguments:
- tokens: bfloat16 [16384, 768], P('expert', 'hidden'), may hold values from -6 to 6
- routes: int32 [16384, 1], P('expert'), may hold values from 0 to 127; in each aligned block of 512 rows (0 to 511, 512 to 1023, ...) at most 8 rows name the same one
- gate_value: float32 [16384, 1], P('expert'), may hold values from 0.2 to 1
- weight_in: bfloat16 [128, 768, 3072], P('expert', None, 'hidden'), may hold values from -0.21875 to 0.21875
- weight_out: bfloat16 [128, 3072, 768], P('expert', 'hidden'), may hold values from -0.109375 to 0.109375
- cotangent: bfloat16 [16384, 768], P('expert', 'hidden'), may hold values from -6 to 6
Outputs:
- layer_out: bfloat16 [16384, 768], P('expert', 'hidden')
- grad_tokens: bfloat16 [16384, 768], P('expert', 'hidden')
- grad_weight_in: bfloat16 [128, 768, 3072], P('expert', None, 'hidden')
- grad_weight_out: bfloat16 [128, 3072, 768], P('expert', 'hidden')
The draws below stay inside these ranges and needn't reach their ends.
Inputs may be any that keep to these rules, and one draw needn't show every extreme that they name: `routes`: within each group of 512 consecutive tokens (the tokens of one index of the expert axis) no expert is chosen by more than 8 tokens; in some group some expert is chosen by exactly 8. Every expert is chosen by some token.
All inputs are finite; a program needn't handle non-finite values.
Results may differ from the reference program's by a relative error of at most 0.019.
Values may be sent and summed in bfloat16 or wider, within the bound.
A program may use at most 64 MiB of HBM per device.

```python
import math
import jax
import jax.numpy as jnp
import numpy as np
from jax import lax

D = 768
H = 3072
TOK_DEV = 512
EXPERTS = 128
CAP = 8
TOKENS = 16384
N_EXPERT = 32
N_HIDDEN = 16


def level_of(stream_key, shape, cuts, smallest, largest):
    level, own = 1.0, jax.random.fold_in(stream_key, 6)
    for dim, blocks in cuts:
        draws = jnp.exp(jax.random.uniform(jax.random.fold_in(own, dim), (blocks,), jnp.float32, smallest / len(cuts), largest / len(cuts)))
        level = level * jnp.repeat(draws, shape[dim] // blocks).reshape([-1 if axis == dim else 1 for axis in range(len(shape))])
    return level


def routed_block(rng, own, number, rows, amount, top, limit, skew):
    sequence = jax.random.permutation(rng, amount)
    crowded, common = load_shares(amount, rows * top, limit, skew, True), load_shares(amount, rows * top, limit, skew, False)
    places = jnp.arange(amount)

    def named(tallies, rotation):
        used = int((tallies > 0).sum())
        fixed = max(1, used // 4)
        moved = fixed + (places - fixed + rotation * (used - fixed)) % max(1, amount - fixed)
        return jnp.zeros((amount,), jnp.int32).at[sequence[jnp.where(places < fixed, places, moved)]].set(jnp.asarray(tallies, jnp.int32))

    tallies = jnp.where(number % 4 == 0, named(crowded, number // 4), named(common, number - number // 4 - 1))
    mixed = jax.random.permutation(jax.random.fold_in(own, 3), amount)
    source_of, sink = mixed[0:amount // 2 * 2:2], mixed[1:amount // 2 * 2:2]
    margin = jnp.minimum(tallies[source_of] - 1, limit - tallies[sink]) // 2
    margin = jnp.where((source_of == sequence[0]) | (sink == sequence[0]) | (tallies[sink] == 0), 0, jnp.maximum(margin, 0))
    moved = jax.random.randint(jax.random.fold_in(own, 4), (amount // 2,), 0, 1 << 20) % (margin + 1)
    tallies = tallies.at[source_of].add(-moved).at[sink].add(moved)
    members = jnp.searchsorted(jnp.cumsum(tallies), jnp.arange(rows * top), side="right").astype(jnp.int32)
    table = members.reshape(top, rows).T
    table = table[jax.random.permutation(jax.random.fold_in(own, 1), rows)]
    rotation = jax.random.randint(jax.random.fold_in(own, 2), (rows, 1), 0, top)
    return jnp.take_along_axis(table, (jnp.arange(top)[None, :] + rotation) % top, axis=1)


def load_shares(count, total, bound, lean, full):
    weights = [(1 << 20) // math.isqrt(rank ** lean) + 1 for rank in range(1, count + 1)]
    largest = bound if full else min(bound, max(-(-total // count), total * weights[0] // sum(weights)))
    least = 1 if total - largest >= count - 1 else 0
    given, rest = [largest] + [least] * (count - 1), total - largest - least * (count - 1)
    while rest > 0:
        candidates = [i for i in range(1, count) if given[i] < largest] or [i for i in range(1, count) if given[i] < bound]
        mass, remaining = sum([weights[i] for i in candidates]), rest
        for i in candidates:
            extra = min(bound - given[i], max(1, remaining * weights[i] // mass), rest)
            given[i] = given[i] + extra
            rest = rest - extra
    return np.array(given)


def normal_values(own_key, extent, scale, bound, split=(), kind=jnp.bfloat16):
    drawn = scale * jax.random.normal(own_key, extent, jnp.float32)
    if split:
        drawn = drawn * level_of(own_key, extent, split, -0.22, 0.18)
    return jnp.clip(drawn, -bound, bound).astype(kind)


def setup_inputs(seed: int = 0) -> dict:
    key_of = jax.random.split(jax.random.key(seed), 7)
    tokens = normal_values(key_of[0], (TOKENS, D), 1.0, 6.0, ((0, 32), (1, 16)))
    routes_keys = jax.random.split(jax.random.fold_in(key_of[1], 1), TOKENS // TOK_DEV)
    routes_turns = jax.random.permutation(jax.random.fold_in(key_of[1], 3), TOKENS // TOK_DEV)
    routes = jax.vmap(lambda own, number: routed_block(jax.random.fold_in(key_of[1], 2), own, number, TOK_DEV, EXPERTS, 1, CAP, 2))(routes_keys, routes_turns).reshape((TOKENS, 1))
    gate_value = jnp.clip(0.2 + 0.8 * jax.random.uniform(key_of[2], (TOKENS, 1), jnp.float32) ** level_of(key_of[2], (TOKENS, 1), ((0, 32),), -0.2, 0.2), 0.2, 1.0)
    weight_in = normal_values(key_of[3], (EXPERTS, D, H), D ** -0.5, 0.21875, ((0, 32), (2, 16)))
    weight_out = normal_values(key_of[4], (EXPERTS, H, D), H ** -0.5, 0.109375, ((0, 32), (1, 16)))
    cotangent = normal_values(key_of[5], (TOKENS, D), 1.0, 6.0, ((0, 32), (1, 16)))
    return dict(tokens=tokens, routes=routes, gate_value=gate_value, weight_in=weight_in, weight_out=weight_out, cotangent=cotangent)


def gelu_tanh(values):
    return jax.nn.gelu(values, approximate=True)

def slot_places(routes):
    chosen = routes[:, 0].reshape(N_EXPERT, TOK_DEV)
    matches = (chosen[:, :, None] == jnp.arange(EXPERTS, dtype=jnp.int32)[None, None, :]).astype(jnp.int32)
    before = jnp.cumsum(matches, axis=1) - matches
    within = lax.optimization_barrier(jnp.sum(before * matches, axis=2))
    source = jnp.arange(N_EXPERT, dtype=jnp.int32)[:, None]
    return (chosen * (N_EXPERT * CAP) + source * CAP + within).reshape(TOKENS).astype(jnp.int32)

def shard_sum(partials):
    rounded = lax.optimization_barrier(partials.astype(jnp.bfloat16))
    return lax.optimization_barrier(jnp.sum(rounded.astype(jnp.float32), axis=0))

def one_expert(inputs):
    rows_in, rows_grad, first_weight, second_weight = inputs
    count = rows_in.shape[0]
    width = H // N_HIDDEN
    preact = jnp.dot(rows_in, first_weight, preferred_element_type=jnp.float32)
    activation, pullback = jax.vjp(gelu_tanh, preact)
    hidden_act = activation.astype(jnp.bfloat16)
    hidden_blocks = hidden_act.reshape(count, N_HIDDEN, width).astype(jnp.float32)
    second_blocks = second_weight.reshape(N_HIDDEN, width, D).astype(jnp.float32)
    expert_out = shard_sum(jnp.einsum('rnh,nhd->nrd', hidden_blocks, second_blocks)).astype(jnp.bfloat16)
    grad_hidden = jnp.dot(rows_grad, second_weight.T, preferred_element_type=jnp.float32)
    grad_pre = pullback(grad_hidden)[0].astype(jnp.bfloat16)
    grad_blocks = grad_pre.reshape(count, N_HIDDEN, width).astype(jnp.float32)
    first_blocks = first_weight.reshape(D, N_HIDDEN, width).astype(jnp.float32)
    expert_grad = shard_sum(jnp.einsum('rnh,dnh->nrd', grad_blocks, first_blocks)).astype(jnp.bfloat16)
    grad_first = jnp.dot(rows_in.T, grad_pre, preferred_element_type=jnp.float32).astype(jnp.bfloat16)
    grad_second = jnp.dot(hidden_act.T, rows_grad, preferred_element_type=jnp.float32).astype(jnp.bfloat16)
    return (expert_out, expert_grad, grad_first, grad_second)

def reference(tokens, routes, gate_value, weight_in, weight_out, cotangent):
    placed = slot_places(routes)
    total = EXPERTS * N_EXPERT * CAP
    scaled = (gate_value * cotangent.astype(jnp.float32)).astype(jnp.bfloat16)
    slot_in = jnp.zeros((total, D), jnp.bfloat16).at[placed].set(tokens).reshape(EXPERTS, N_EXPERT * CAP, D)
    slot_grad = jnp.zeros((total, D), jnp.bfloat16).at[placed].set(scaled).reshape(EXPERTS, N_EXPERT * CAP, D)
    expert_out, expert_grad, grad_weight_in, grad_weight_out = lax.map(one_expert, (slot_in, slot_grad, weight_in, weight_out))
    layer_out = (gate_value * expert_out.reshape(total, D)[placed].astype(jnp.float32)).astype(jnp.bfloat16)
    grad_tokens = expert_grad.reshape(total, D)[placed]
    return (layer_out, grad_tokens, grad_weight_in, grad_weight_out)
```

```python
import functools

import jax
import jax.numpy as jnp
from jax import lax
from jax.experimental import pallas as pl
from jax.experimental.pallas import tpu as pltpu
from jax.sharding import PartitionSpec as P

MESH = pl.DeviceIdType.MESH
RING = 4
CORES = 2
CAP = 8
PAIR = 2
CHUNKS = 2
LANES = 128
F32 = jnp.float32
BF16 = jnp.bfloat16
NN = (((1,), (0,)), ((), ()))
NT = (((1,), (1,)), ((), ()))

PLACES = (0, -1, 1, 2)
ARRIVALS = [(-1, 0, None), (1, 0, None), (2, 0, 0), (2, 0, 1)]
for _i in PLACES:
    ARRIVALS += [(_i, -1, None), (_i, 1, None), (_i, 2, 0), (_i, 2, 1)]
ARRIVAL = {name: number for number, name in enumerate(ARRIVALS)}
ITEM = {2: 0, 1: 1, -1: 2, 0: 3}


def near(place):
    return (place + 1) % RING - 1


def dot(a, b, dims=NN):
    return lax.dot_general(a, b, dims, preferred_element_type=F32)


def gelu_and_slope(v):
    c = 0.7978845608028654
    square = v * v
    t = jnp.tanh(c * (v + 0.044715 * v * square))
    half = 0.5 * (1.0 + t)
    slope = half + 0.5 * v * (1.0 - t * t) * (c + c * 3.0 * 0.044715 * square)
    return v * half, slope


def kernel(
    tokens_ref, routes_ref, gate_ref, wint_ref, wout_ref, cot_ref,
    layer_ref, gtok_ref, gwint_ref, gwout_ref,
    chosen_v, send_v, recv_v, bsend_v, back_v, xg_v, part_v, via_v, frm_v,
    wint_v, wout_v, win_v, woutt_v, hid_v, gp_v, gwint_v, gwout_v,
    w_sem, gw_sem, a2a_send, a2a_recv, back_send, back_recv,
    ag_send, ag_recv, rs_send, via_recv, frm_recv,
):
    owners = lax.axis_size("expert")
    feat, tok = tokens_ref.shape
    exp_dev, units, width = wint_ref.shape
    rows = PAIR * CAP
    length = owners * rows
    half = length // 2
    chips = owners // CORES
    me = lax.axis_index("expert")
    here = lax.axis_index("hidden")
    x, y = here // RING, lax.rem(here, RING)

    def hidden_at(dx, dy):
        return lax.rem(x + dx + RING, RING) * RING + lax.rem(y + dy + RING, RING)

    def place(part, i, j):
        return hidden_at(i, j) if part == 0 else hidden_at(j, i)

    def neighbour(part, axis, step):
        return (me, place(part, step, 0) if axis == 0 else place(part, 0, step))

    wint_copy = pltpu.make_async_copy(wint_ref, wint_v, w_sem.at[0])
    wout_copy = pltpu.make_async_copy(wout_ref, wout_v, w_sem.at[1])
    wint_copy.start()
    wout_copy.start()
    barrier = pltpu.get_barrier_semaphore()

    def greet(i, carry):
        pl.semaphore_signal(barrier, inc=1, device_id=(lax.rem(me + i, owners), here), device_id_type=MESH)
        return carry

    lax.fori_loop(1, owners, greet, 0)
    for step in (1, -1):
        for axis in (0, 1):
            pl.semaphore_signal(barrier, inc=1, device_id=neighbour(0, axis, step), device_id_type=MESH)

    routes = routes_ref[...]
    experts = owners * exp_dev
    matches = jnp.where(routes == lax.broadcasted_iota(jnp.int32, (experts, tok), 0), 1.0, 0.0)
    earlier = jnp.where(
        lax.broadcasted_iota(jnp.int32, (tok, tok), 0) < lax.broadcasted_iota(jnp.int32, (tok, tok), 1), 1.0, 0.0
    ).astype(BF16)
    before = dot(matches.astype(BF16), earlier)
    slot = jnp.sum(before * matches, axis=0, keepdims=True).astype(jnp.int32)
    within = routes & (exp_dev - 1)
    pos = (within // PAIR) * length + (routes // exp_dev) * rows + (within & (PAIR - 1)) * CAP + slot
    scaled = gate_ref[...] * cot_ref[...].astype(F32)
    empty = jnp.zeros((LANES - 2 * feat, tok), BF16)
    both = jnp.concatenate([tokens_ref[...], scaled.astype(BF16), empty], axis=0)
    for p in range(CHUNKS):
        chosen_v[p] = jnp.where(
            lax.broadcasted_iota(jnp.int32, (length, tok), 0) + p * length == pos, 1.0, 0.0
        ).astype(BF16)
        send_v[p] = dot(chosen_v[p], both, NT).astype(BF16)

    pl.semaphore_wait(barrier, owners - 1 + 4)

    def exchange(src, dst, send_sem, recv_sem):
        def one(to):
            pltpu.make_async_remote_copy(
                src_ref=src.at[pl.ds(pl.multiple_of(to * rows, rows), rows)],
                dst_ref=dst.at[pl.ds(pl.multiple_of(me * rows, rows), rows)],
                send_sem=send_sem, recv_sem=recv_sem, device_id=(to, here), device_id_type=MESH,
            ).start()

        def chip(i, carry):
            distance = chips // 2 - (i + 1) // 2
            step = jnp.where(lax.rem(i, 2) == 1, distance, chips - distance)
            for other in range(CORES):
                one(lax.rem((me // CORES + step) * CORES + lax.rem(me + other, CORES), owners))
            return carry

        lax.fori_loop(0, chips - 1, chip, 0)
        one((me // CORES) * CORES + 1 - lax.rem(me, CORES))
        mine = pl.ds(pl.multiple_of(me * rows, rows), rows)
        dst[mine, :] = src[mine, :]

    def exchange_wait(ref, sem):
        view = ref.at[pl.ds(0, length - rows)]
        pltpu.make_async_copy(view, view, sem).wait()

    for p in range(CHUNKS):
        exchange(send_v.at[p], recv_v.at[p], a2a_send.at[p], a2a_recv.at[p])

    wint_copy.wait()
    wout_copy.wait()
    for e in range(exp_dev):
        win_v[e] = jnp.transpose(wint_v[e])
        woutt_v[e] = jnp.transpose(wout_v[e])

    def lanes_of(ref, which):
        return ref if which is None else ref.at[:, pl.ds(which * half, half)]

    def ag_copy(part, p, i, j, which, axis, step):
        ref = lanes_of(xg_v.at[part, p, place(part, i, j)], which)
        there = (near(i - step), j, which) if axis == 0 else (i, near(j - step), which)
        return pltpu.make_async_remote_copy(
            src_ref=ref, dst_ref=ref, send_sem=ag_send.at[part, p],
            recv_sem=ag_recv.at[part, p, ARRIVAL[there]],
            device_id=neighbour(part, axis, step), device_id_type=MESH,
        )

    def ag_send_to(part, p, i, j, which, axis, step):
        ag_copy(part, p, i, j, which, axis, step).start()

    def ag_wait(part, p, i, j, which=None):
        ref = lanes_of(xg_v.at[part, p, place(part, i, j)], which)
        pltpu.make_async_copy(ref, ref, ag_recv.at[part, p, ARRIVAL[(i, j, which)]]).wait()

    def ag_start(p):
        exchange_wait(recv_v.at[p], a2a_recv.at[p])
        arrived = recv_v[p].astype(F32).reshape(owners, PAIR, CAP, LANES)
        for e in range(PAIR):
            turned = jnp.transpose(arrived[:, e].reshape(half, LANES))
            for part in range(2):
                xg_v[part, p, here, :, e * half:(e + 1) * half] = turned[part * feat:(part + 1) * feat].astype(BF16)
        for axis in (0, 1):
            for step in (1, -1):
                for part in range(2):
                    ag_send_to(part, p, 0, 0, None, axis, step)

    def ag_first(p):
        for which, step in ((0, 1), (1, -1)):
            for part in range(2):
                ag_wait(part, p, -step, 0)
                ag_send_to(part, p, -step, 0, which, 0, step)
                for up in (1, -1):
                    ag_send_to(part, p, -step, 0, None, 1, up)

    def ag_row(p, i):
        for which, step in ((0, 1), (1, -1)):
            for part in range(2):
                ag_wait(part, p, i, -step)
                ag_send_to(part, p, i, -step, which, 1, step)

    def ag_second(p):
        for part in range(2):
            for which in range(2):
                ag_wait(part, p, 2, 0, which)
            for up in (1, -1):
                ag_send_to(part, p, 2, 0, None, 1, up)

    def ag_end(p):
        for i in PLACES:
            for part in range(2):
                for which in range(2):
                    ag_wait(part, p, i, 2, which)

    def forward_backward(p, e):
        expert = p * PAIR + e
        span = slice(e * half, (e + 1) * half)
        rows_x = xg_v[0, p, :, :, span].reshape(width, half)
        rows_g = xg_v[1, p, :, :, span].reshape(width, half)
        act, slope = gelu_and_slope(dot(wint_v[expert], rows_x))
        act = act.astype(BF16)
        hid_v[expert] = act
        part_v[0, p, :, :, span] = dot(woutt_v[expert], act).astype(BF16).reshape(width // feat, feat, half)
        grad = (dot(wout_v[expert], rows_g) * slope).astype(BF16)
        gp_v[expert] = grad
        part_v[1, p, :, :, span] = dot(win_v[expert], grad).astype(BF16).reshape(width // feat, feat, half)

    def weight_grads(p, e):
        expert = p * PAIR + e
        span = slice(e * half, (e + 1) * half)
        rows_x = xg_v[0, p, :, :, span].reshape(width, half)
        rows_g = xg_v[1, p, :, :, span].reshape(width, half)
        gwint_v[expert] = dot(gp_v[expert], rows_x, NT).astype(BF16)
        pltpu.make_async_copy(gwint_v.at[expert], gwint_ref.at[expert], gw_sem.at[0, expert]).start()
        gwout_v[expert] = dot(hid_v[expert], rows_g, NT).astype(BF16)
        pltpu.make_async_copy(gwout_v.at[expert], gwout_ref.at[expert], gw_sem.at[1, expert]).start()

    def rs_copy(part, p, i, j, which, axis, step, item, through):
        ref = lanes_of(part_v.at[part, p, place(part, i, j)], which)
        number = 0 if step == 1 else 1
        if through:
            dst, sem = via_v.at[part, p, item, number], via_recv.at[part, p, item, number]
        else:
            dst, sem = lanes_of(frm_v.at[part, p, item, number], which), frm_recv.at[part, p, item, number]
        pltpu.make_async_remote_copy(
            src_ref=ref, dst_ref=dst, send_sem=rs_send.at[part, p], recv_sem=sem,
            device_id=neighbour(part, axis, step), device_id_type=MESH,
        ).start()

    def rs_start(p, which):
        step = 1 if which == 0 else -1
        for i, item in ITEM.items():
            for part in range(2):
                rs_copy(part, p, i, 2, which, 1, step, item, True)
            for part in range(2):
                rs_copy(part, p, i, -step, which, 1, -step, item, False)

    def add_via(part, p, i, j, which, item):
        number = which
        buf = via_v.at[part, p, item, number]
        pltpu.make_async_copy(buf, buf, via_recv.at[part, p, item, number]).wait()
        ref = lanes_of(part_v.at[part, p, place(part, i, j)], which)
        ref[...] = (ref[...].astype(F32) + buf[...].astype(F32)).astype(BF16)

    def rs_middle(p, i):
        item = ITEM[i]
        for which, step in ((0, 1), (1, -1)):
            for part in range(2):
                add_via(part, p, i, step, which, item)
                rs_copy(part, p, i, step, which, 1, step, item, False)

    def total_of(part, p, i, item):
        total = part_v[part, p, place(part, i, 0)].astype(F32)
        for number in range(2):
            buf = frm_v.at[part, p, item, number]
            pltpu.make_async_copy(buf, buf, frm_recv.at[part, p, item, number]).wait()
            total = total + buf[...].astype(F32)
        return total.astype(BF16)

    def rs_sum(p, i):
        for part in range(2):
            part_v[part, p, place(part, i, 0)] = total_of(part, p, i, ITEM[i])
            if i == 2:
                rs_copy(part, p, i, 0, 0, 0, 1, 4, True)
                rs_copy(part, p, i, 0, 1, 0, -1, 4, True)
            elif i == 1:
                rs_copy(part, p, i, 0, 1, 0, 1, 4, False)
            elif i == -1:
                rs_copy(part, p, i, 0, 0, 0, -1, 4, False)

    def rs_last(p):
        for which, step in ((0, 1), (1, -1)):
            for part in range(2):
                add_via(part, p, step, 0, which, 4)
                rs_copy(part, p, step, 0, which, 0, step, 4, False)

    def rs_end(p):
        totals = [total_of(part, p, 0, 4).astype(F32) for part in range(2)]
        totals.append(jnp.zeros((LANES - 2 * feat, length), F32))
        turned = jnp.transpose(jnp.concatenate(totals, axis=0)).reshape(PAIR, owners, CAP, LANES)
        turned = jnp.concatenate([turned[e][:, None] for e in range(PAIR)], axis=1)
        bsend_v[p] = turned.reshape(length, LANES).astype(BF16)
        exchange(bsend_v.at[p], back_v.at[p], back_send.at[p], back_recv.at[p])

    ag_start(0)
    ag_first(0)
    ag_row(0, 0)
    ag_second(0)
    ag_row(0, -1)
    ag_start(1)
    ag_row(0, 1)
    ag_row(0, 2)
    ag_first(1)
    ag_row(1, 0)
    ag_second(1)
    ag_end(0)
    forward_backward(0, 0)
    rs_start(0, 0)
    ag_row(1, -1)
    ag_row(1, 1)
    ag_row(1, 2)
    forward_backward(0, 1)
    rs_start(0, 1)
    weight_grads(0, 0)
    weight_grads(0, 1)
    ag_end(1)
    forward_backward(1, 0)
    rs_start(1, 0)
    forward_backward(1, 1)
    rs_start(1, 1)
    for i in ITEM:
        rs_middle(0, i)
    for i in ITEM:
        rs_sum(0, i)
    weight_grads(1, 0)
    weight_grads(1, 1)
    rs_last(0)
    for i in ITEM:
        rs_middle(1, i)
    rs_end(0)
    for i in ITEM:
        rs_sum(1, i)
    rs_last(1)
    rs_end(1)

    taken = jnp.zeros((LANES, tok), F32)
    for p in range(CHUNKS):
        exchange_wait(back_v.at[p], back_recv.at[p])
        turned = jnp.transpose(back_v[p].astype(F32)).astype(BF16)
        taken = taken + dot(turned, chosen_v[p])
    layer_ref[...] = (gate_ref[...] * taken[0:feat]).astype(BF16)
    gtok_ref[...] = taken[feat:2 * feat].astype(BF16)

    for expert in range(exp_dev):
        pltpu.make_async_copy(gwint_v.at[expert], gwint_ref.at[expert], gw_sem.at[0, expert]).wait()
        pltpu.make_async_copy(gwout_v.at[expert], gwout_ref.at[expert], gw_sem.at[1, expert]).wait()
    for p in range(CHUNKS):
        exchange_wait(send_v.at[p], a2a_send.at[p])
        exchange_wait(bsend_v.at[p], back_send.at[p])
        for part in range(2):
            for buf, sem in ((xg_v, ag_send), (part_v, rs_send)):
                view = buf.at[part, p, pl.ds(0, RING * RING - 1)]
                pltpu.make_async_copy(view, view, sem.at[part, p]).wait()


def local(tokens, routes, gate_value, weight_in, weight_out, cotangent):
    owners = lax.axis_size("expert")
    blocks = lax.axis_size("hidden")
    tok, feat = tokens.shape
    exp_dev, width, units = weight_in.shape
    length = owners * PAIR * CAP
    half = length // 2
    vmem = pl.BlockSpec(memory_space=pltpu.VMEM)
    hbm = pl.BlockSpec(memory_space=pl.ANY)
    dma = pltpu.SemaphoreType.DMA
    weights = pltpu.VMEM((exp_dev, units, width), BF16)
    turned_weights = pltpu.VMEM((exp_dev, width, units), BF16)
    rows = pltpu.VMEM((CHUNKS, length, LANES), BF16)
    layer_out, grad_tokens, grad_in, grad_out = pl.pallas_call(
        kernel,
        out_shape=(
            jax.ShapeDtypeStruct((feat, tok), BF16),
            jax.ShapeDtypeStruct((feat, tok), BF16),
            jax.ShapeDtypeStruct((exp_dev, units, width), BF16),
            jax.ShapeDtypeStruct((exp_dev, units, width), BF16),
        ),
        in_specs=[vmem, vmem, vmem, hbm, hbm, vmem],
        out_specs=(vmem, vmem, hbm, hbm),
        scratch_shapes=[
            pltpu.VMEM((CHUNKS, length, tok), BF16),
            rows, rows, rows, rows,
            pltpu.VMEM((2, CHUNKS, blocks, feat, length), BF16),
            pltpu.VMEM((2, CHUNKS, blocks, feat, length), BF16),
            pltpu.VMEM((2, CHUNKS, 5, 2, feat, half), BF16),
            pltpu.VMEM((2, CHUNKS, 5, 2, feat, length), BF16),
            weights, weights, turned_weights, turned_weights,
            pltpu.VMEM((exp_dev, units, half), BF16),
            pltpu.VMEM((exp_dev, units, half), BF16),
            weights, weights,
            dma((2,)),
            dma((2, exp_dev)),
            dma((CHUNKS,)),
            dma((CHUNKS,)),
            dma((CHUNKS,)),
            dma((CHUNKS,)),
            dma((2, CHUNKS)),
            dma((2, CHUNKS, len(ARRIVALS))),
            dma((2, CHUNKS)),
            dma((2, CHUNKS, 5, 2)),
            dma((2, CHUNKS, 5, 2)),
        ],
        compiler_params=pltpu.CompilerParams(
            collective_id=0, has_side_effects=True, vmem_limit_bytes=60 * 1024 * 1024
        ),
        name="expert_layer",
    )(tokens.T, routes.T, gate_value.T, weight_in.transpose(0, 2, 1), weight_out, cotangent.T)
    return layer_out.T, grad_tokens.T, grad_in.transpose(0, 2, 1), grad_out


def solution(mesh):
    in_specs = (
        P("expert", "hidden"),
        P("expert", None),
        P("expert", None),
        P("expert", None, "hidden"),
        P("expert", "hidden", None),
        P("expert", "hidden"),
    )
    out_specs = (
        P("expert", "hidden"),
        P("expert", "hidden"),
        P("expert", None, "hidden"),
        P("expert", "hidden", None),
    )
    return jax.shard_map(local, mesh=mesh, in_specs=in_specs, out_specs=out_specs, check_vma=False)
```

```python
import functools

import jax
import jax.numpy as jnp
from jax import lax
from jax.experimental import pallas as pl
from jax.experimental.pallas import tpu as pltpu
from jax.sharding import PartitionSpec as P

MESH = pl.DeviceIdType.MESH
RING = 4
CORES = 2
CAP = 8
PAIR = 2
SIDES = 2
CHUNKS = 4
LANES = 128
F32 = jnp.float32
BF16 = jnp.bfloat16
NN = (((1,), (0,)), ((), ()))
NT = (((1,), (1,)), ((), ()))

PLACES = (0, -1, 1, 2)
ARRIVALS = [(-1, 0, None), (1, 0, None), (2, 0, None)]
for _i in PLACES:
    ARRIVALS += [(_i, -1, None), (_i, 1, None), (_i, 2, 0), (_i, 2, 1)]
ARRIVAL = {name: number for number, name in enumerate(ARRIVALS)}
ITEM = {2: 0, 1: 1, -1: 2, 0: 3}

ORDER = (
    ("S", 0), ("S", 1), ("F", 0, -1), ("F", 0, 1), ("R", 0, 0), ("F", 0, 2), ("F", 1, -1), ("F", 1, 1),
    ("S", 2), ("R", 1, 0), ("F", 1, 2), ("R", 0, -1), ("R", 0, 1), ("R", 0, 2), ("R", 1, -1), ("R", 1, 1),
    ("F", 2, -1), ("S", 3), ("F", 2, 1), ("R", 2, 0), ("F", 2, 2), ("R", 1, 2), ("R", 2, -1), ("F", 3, -1),
    ("F", 3, 1), ("R", 3, 0), ("F", 3, 2), ("R", 2, 1), ("R", 2, 2), ("C", 1, 0), ("C", 1, 1), ("R", 3, -1),
    ("R", 3, 1), ("R", 3, 2), ("C", 2, 0), ("C", 2, 1), ("M", 1, 2), ("M", 1, 1), ("M", 1, -1), ("M", 1, 0),
    ("C", 3, 0), ("C", 3, 1), ("M", 2, 2), ("M", 2, 1), ("M", 2, -1), ("M", 2, 0), ("U", 1, 2), ("U", 1, 1),
    ("U", 1, -1), ("C", 0, 0), ("C", 0, 1), ("M", 3, 1), ("M", 3, -1), ("M", 3, 2), ("M", 3, 0), ("U", 2, 2),
    ("U", 2, 1), ("U", 2, -1), ("Z", 1), ("M", 0, 2), ("M", 0, 1), ("M", 0, -1), ("M", 0, 0), ("U", 3, 1),
    ("U", 3, -1), ("U", 3, 2), ("Z", 2), ("U", 0, 2), ("U", 0, 1), ("U", 0, -1), ("Z", 3), ("Z", 0),
)


def near(place):
    return (place + 1) % RING - 1


def dot(a, b, dims=NN):
    return lax.dot_general(a, b, dims, preferred_element_type=F32)


def gelu_and_slope(v):
    c = 0.7978845608028654
    square = v * v
    t = jnp.tanh(c * (v + 0.044715 * v * square))
    half = 0.5 * (1.0 + t)
    slope = half + 0.5 * v * (1.0 - t * t) * (c + c * 3.0 * 0.044715 * square)
    return v * half, slope


def kernel(
    tokens_ref, routes_ref, gate_ref, wint_ref, wout_ref, cot_ref,
    layer_ref, gtok_ref, gwint_ref, gwout_ref,
    chosen_v, send_v, recv_v, bsend_v, back_v, xg_v, part_v, via_v, frm_v, last_v,
    wint_v, wout_v, win_v, woutt_v, hid_v, gp_v, gwint_v, gwout_v,
    w_sem, gw_sem, a2a_send, a2a_recv, back_send, back_recv,
    ag_send, ag_recv, rs_send, via_recv, frm_recv, last_recv,
):
    owners = lax.axis_size("expert")
    feat, tok = tokens_ref.shape
    exp_dev, units, width = wint_ref.shape
    rows = PAIR * CAP
    length = owners // SIDES * rows
    half = length // PAIR
    chips = owners // CORES
    behind = max(chips // 4 - 1, 0)
    me = lax.axis_index("expert")
    here = lax.axis_index("hidden")
    x, y = here // RING, lax.rem(here, RING)

    def hidden_at(dx, dy):
        return lax.rem(x + dx + RING, RING) * RING + lax.rem(y + dy + RING, RING)

    def place(part, i, j):
        return hidden_at(i, j) if part == 0 else hidden_at(j, i)

    def neighbour(part, axis, step):
        return (me, place(part, step, 0) if axis == 0 else place(part, 0, step))

    wint_copy = pltpu.make_async_copy(wint_ref, wint_v, w_sem.at[0])
    wout_copy = pltpu.make_async_copy(wout_ref, wout_v, w_sem.at[1])
    wint_copy.start()
    wout_copy.start()
    barrier = pltpu.get_barrier_semaphore()

    def greet(i, carry):
        pl.semaphore_signal(barrier, inc=1, device_id=(lax.rem(me + i, owners), here), device_id_type=MESH)
        return carry

    lax.fori_loop(1, owners, greet, 0)
    for step in (1, -1, 2):
        for axis in (0, 1):
            pl.semaphore_signal(barrier, inc=1, device_id=neighbour(0, axis, step), device_id_type=MESH)

    routes = routes_ref[...]
    experts = owners * exp_dev
    matches = jnp.where(routes == lax.broadcasted_iota(jnp.int32, (experts, tok), 0), 1.0, 0.0)
    earlier = jnp.where(
        lax.broadcasted_iota(jnp.int32, (tok, tok), 0) < lax.broadcasted_iota(jnp.int32, (tok, tok), 1), 1.0, 0.0
    ).astype(BF16)
    before = dot(matches.astype(BF16), earlier)
    slot = jnp.sum(before * matches, axis=0, keepdims=True).astype(jnp.int32)
    pos = routes * CAP + slot
    scaled = gate_ref[...] * cot_ref[...].astype(F32)
    empty = jnp.zeros((LANES - 2 * feat, tok), BF16)
    both = jnp.concatenate([tokens_ref[...], scaled.astype(BF16), empty], axis=0)
    chosen_v[...] = jnp.where(
        lax.broadcasted_iota(jnp.int32, chosen_v.shape, 0) == pos, 1.0, 0.0
    ).astype(BF16)
    send_v[...] = dot(chosen_v[...], both, NT).astype(BF16)

    pl.semaphore_wait(barrier, owners - 1 + 6)

    chip, core = me // CORES, lax.rem(me, CORES)
    side_chips = chips // SIDES
    pairs = exp_dev // PAIR

    def block(number):
        return pl.ds(pl.multiple_of(number * rows, rows), rows)

    def exchange(c, outward, src, dst, send_sem, recv_sem):
        side, pair = c // pairs, c % pairs
        for number in sorted(
            range(side_chips), key=lambda k: -min((side * side_chips + k - behind) % chips, (behind - side * side_chips - k) % chips)
        ):
            ahead = side * side_chips + number - behind
            way = -ahead if outward else ahead
            for other in range(CORES):
                to_core = lax.rem(core + other, CORES)
                to = lax.rem(chip + way + chips, chips) * CORES + to_core
                if outward:
                    take, put = to * pairs + pair, (c * side_chips + number) * CORES + core
                else:
                    take, put = (c * side_chips + number) * CORES + to_core, me * pairs + pair
                if ahead == 0 and other == 0:
                    dst[block(put), :] = src[block(take), :]
                else:
                    pltpu.make_async_remote_copy(
                        src_ref=src.at[block(take)], dst_ref=dst.at[block(put)],
                        send_sem=send_sem.at[c], recv_sem=recv_sem.at[c], device_id=(to, here), device_id_type=MESH,
                    ).start()

    def exchange_wait(c, ref, sem):
        view = ref.at[pl.ds(0, length - rows if c // pairs == 0 else length)]
        pltpu.make_async_copy(view, view, sem.at[c]).wait()

    for c in range(CHUNKS):
        exchange(c, True, send_v, recv_v, a2a_send, a2a_recv)

    wint_copy.wait()
    wout_copy.wait()
    for e in range(exp_dev):
        win_v[e] = jnp.transpose(wint_v[e])
        woutt_v[e] = jnp.transpose(wout_v[e])

    def lanes_of(ref, which):
        return ref if which is None else ref.at[:, pl.ds(which * half, half)]

    def ag_copy(part, p, i, j, which, axis, step):
        ref = lanes_of(xg_v.at[part, p, place(part, i, j)], which)
        there = (near(i - step), j, which) if axis == 0 else (i, near(j - step), which)
        return pltpu.make_async_remote_copy(
            src_ref=ref, dst_ref=ref, send_sem=ag_send.at[part, p],
            recv_sem=ag_recv.at[part, p, ARRIVAL[there]],
            device_id=neighbour(part, axis, step), device_id_type=MESH,
        )

    def ag_send_to(part, p, i, j, which, axis, step):
        ag_copy(part, p, i, j, which, axis, step).start()

    def ag_wait(part, p, i, j, which=None):
        ref = lanes_of(xg_v.at[part, p, place(part, i, j)], which)
        pltpu.make_async_copy(ref, ref, ag_recv.at[part, p, ARRIVAL[(i, j, which)]]).wait()

    def ag_start(p):
        exchange_wait(p, recv_v, a2a_recv)
        arrived = recv_v[p * length:(p + 1) * length].astype(F32).reshape(length // rows, PAIR, CAP, LANES)
        for e in range(PAIR):
            turned = jnp.transpose(arrived[:, e].reshape(half, LANES))
            for part in range(2):
                xg_v[part, p, here, :, e * half:(e + 1) * half] = turned[part * feat:(part + 1) * feat].astype(BF16)
        for axis, step in ((0, 1), (0, -1), (0, 2), (1, 1), (1, -1)):
            for part in range(2):
                ag_send_to(part, p, 0, 0, None, axis, step)

    def ag_column(p, i):
        for part in range(2):
            ag_wait(part, p, i, 0)
            for step in (1, -1):
                ag_send_to(part, p, i, 0, None, 1, step)

    def ag_row(p, i):
        for which, step in ((0, 1), (1, -1)):
            for part in range(2):
                ag_wait(part, p, i, -step)
                ag_send_to(part, p, i, -step, which, 1, step)

    def ag_end(p):
        for i in PLACES:
            for part in range(2):
                for which in range(2):
                    ag_wait(part, p, i, 2, which)

    def rows_of(part, p, which):
        return xg_v[part, p, :, :, which * half:(which + 1) * half].reshape(width, half)

    def forward_backward(p, which):
        side, e = p // pairs, p % pairs * PAIR + which
        at, own = slice(which * half, (which + 1) * half), slice(side * half, (side + 1) * half)
        act, slope = gelu_and_slope(dot(wint_v[e], rows_of(0, p, which)))
        act = act.astype(BF16)
        hid_v[e, :, own] = act
        part_v[0, p, :, :, at] = dot(woutt_v[e], act).astype(BF16).reshape(width // feat, feat, half)
        grad = (dot(wout_v[e], rows_of(1, p, which)) * slope).astype(BF16)
        gp_v[e, :, own] = grad
        part_v[1, p, :, :, at] = dot(win_v[e], grad).astype(BF16).reshape(width // feat, feat, half)

    def weight_grads(e):
        rows_x, rows_g = [
            jnp.concatenate([rows_of(part, side * pairs + e // PAIR, e % PAIR) for side in range(SIDES)], axis=1)
            for part in range(2)
        ]
        gwint_v[e] = dot(gp_v[e], rows_x, NT).astype(BF16)
        pltpu.make_async_copy(gwint_v.at[e], gwint_ref.at[e], gw_sem.at[0, e]).start()
        gwout_v[e] = dot(hid_v[e], rows_g, NT).astype(BF16)
        pltpu.make_async_copy(gwout_v.at[e], gwout_ref.at[e], gw_sem.at[1, e]).start()

    def rs_copy(part, p, i, j, which, axis, step, dst, sem):
        pltpu.make_async_remote_copy(
            src_ref=lanes_of(part_v.at[part, p, place(part, i, j)], which), dst_ref=dst,
            send_sem=rs_send.at[part, p], recv_sem=sem,
            device_id=neighbour(part, axis, step), device_id_type=MESH,
        ).start()

    def rs_through(part, p, i, which, step):
        rs_copy(part, p, i, 2, which, 1, step, via_v.at[part, p, ITEM[i], which], via_recv.at[part, p, ITEM[i], which])

    def rs_to(part, p, i, which, step):
        number = 0 if step == 1 else 1
        dst = lanes_of(frm_v.at[part, p, ITEM[i], number], which)
        rs_copy(part, p, i, step, which, 1, step, dst, frm_recv.at[part, p, ITEM[i], number])

    def rs_start(p, which):
        step = 1 if which == 0 else -1
        for i in ITEM:
            for part in range(2):
                rs_through(part, p, i, which, step)
        for i in ITEM:
            for part in range(2):
                rs_to(part, p, i, which, -step)

    def rs_middle(p, i):
        for which, step in ((0, 1), (1, -1)):
            for part in range(2):
                buf, sem = via_v.at[part, p, ITEM[i], which], via_recv.at[part, p, ITEM[i], which]
                pltpu.make_async_copy(buf, buf, sem).wait()
                ref = lanes_of(part_v.at[part, p, place(part, i, step)], which)
                ref[...] = (ref[...].astype(F32) + buf[...].astype(F32)).astype(BF16)
                rs_to(part, p, i, which, step)

    def rs_total(part, p, i):
        total = part_v[part, p, place(part, i, 0)].astype(F32)
        for number in range(2):
            buf = frm_v.at[part, p, ITEM[i], number]
            pltpu.make_async_copy(buf, buf, frm_recv.at[part, p, ITEM[i], number]).wait()
            total = total + buf[...].astype(F32)
        return total

    def rs_sum(p, i):
        for part in range(2):
            part_v[part, p, place(part, i, 0)] = rs_total(part, p, i).astype(BF16)
            rs_copy(part, p, i, 0, None, 0, i, last_v.at[part, p, ITEM[i]], last_recv.at[part, p, ITEM[i]])

    def rs_last(part, p):
        total = rs_total(part, p, 0)
        for i in (1, -1, 2):
            buf = last_v.at[part, p, ITEM[i]]
            pltpu.make_async_copy(buf, buf, last_recv.at[part, p, ITEM[i]]).wait()
            total = total + buf[...].astype(F32)
        return total.astype(BF16).astype(F32)

    def rs_end(p):
        totals = [rs_last(part, p) for part in range(2)]
        totals.append(jnp.zeros((LANES - 2 * feat, length), F32))
        turned = jnp.transpose(jnp.concatenate(totals, axis=0)).reshape(PAIR, length // rows, CAP, LANES)
        turned = jnp.concatenate([turned[e][:, None] for e in range(PAIR)], axis=1)
        bsend_v[p * length:(p + 1) * length] = turned.reshape(length, LANES).astype(BF16)
        exchange(p, False, bsend_v, back_v, back_send, back_recv)

    def compute(p, which):
        if which == 0:
            ag_end(p)
        forward_backward(p, which)
        rs_start(p, which)

    for step, *on in ORDER:
        {"S": ag_start, "F": ag_column, "R": ag_row, "C": compute, "M": rs_middle, "U": rs_sum, "Z": rs_end}[step](*on)
    for e in range(exp_dev):
        weight_grads(e)

    for p in range(CHUNKS):
        exchange_wait(p, back_v, back_recv)
    turned = jnp.transpose(back_v[...].astype(F32)).astype(BF16)
    taken = dot(turned, chosen_v[...])
    layer_ref[...] = (gate_ref[...] * taken[0:feat]).astype(BF16)
    gtok_ref[...] = taken[feat:2 * feat].astype(BF16)

    for expert in range(exp_dev):
        pltpu.make_async_copy(gwint_v.at[expert], gwint_ref.at[expert], gw_sem.at[0, expert]).wait()
        pltpu.make_async_copy(gwout_v.at[expert], gwout_ref.at[expert], gw_sem.at[1, expert]).wait()
    for p in range(CHUNKS):
        exchange_wait(p, send_v, a2a_send)
        exchange_wait(p, bsend_v, back_send)
        for part in range(2):
            for buf, sem in ((xg_v, ag_send), (part_v, rs_send)):
                view = buf.at[part, p, pl.ds(0, RING * RING - 1)]
                pltpu.make_async_copy(view, view, sem.at[part, p]).wait()


def hand_over(*refs):
    count = (len(refs) - 2) // 3
    given, outs, held = refs[:count], refs[count:2 * count], refs[2 * count:3 * count]
    in_sem, out_sem = refs[3 * count:]
    into = [pltpu.make_async_copy(given[i], held[i], in_sem.at[i]) for i in range(count)]
    out = [pltpu.make_async_copy(held[i], outs[i], out_sem.at[i]) for i in range(count)]
    for copy in into:
        copy.start()
    for i in range(count):
        into[i].wait()
        out[i].start()
    for copy in out:
        copy.wait()


def local(tokens, routes, gate_value, weight_in, weight_out, cotangent):
    owners = lax.axis_size("expert")
    blocks = lax.axis_size("hidden")
    tok, feat = tokens.shape
    exp_dev, width, units = weight_in.shape
    slots = owners * exp_dev * CAP
    length = owners // SIDES * PAIR * CAP
    half = length // PAIR
    vmem = pl.BlockSpec(memory_space=pltpu.VMEM)
    hbm = pl.BlockSpec(memory_space=pl.ANY)
    dma = pltpu.SemaphoreType.DMA
    weights = pltpu.VMEM((exp_dev, units, width), BF16)
    turned_weights = pltpu.VMEM((exp_dev, width, units), BF16)
    rows = pltpu.VMEM((slots, LANES), BF16)
    outs = pl.pallas_call(
        kernel,
        out_shape=(
            jax.ShapeDtypeStruct((feat, tok), BF16),
            jax.ShapeDtypeStruct((feat, tok), BF16),
            jax.ShapeDtypeStruct((exp_dev, units, width), BF16),
            jax.ShapeDtypeStruct((exp_dev, units, width), BF16),
        ),
        in_specs=[vmem, vmem, vmem, hbm, hbm, vmem],
        out_specs=(vmem, vmem, hbm, hbm),
        scratch_shapes=[
            pltpu.VMEM((slots, tok), BF16),
            rows, rows, rows, rows,
            pltpu.VMEM((2, CHUNKS, blocks, feat, length), BF16),
            pltpu.VMEM((2, CHUNKS, blocks, feat, length), BF16),
            pltpu.VMEM((2, CHUNKS, RING, 2, feat, half), BF16),
            pltpu.VMEM((2, CHUNKS, RING, 2, feat, length), BF16),
            pltpu.VMEM((2, CHUNKS, RING - 1, feat, length), BF16),
            weights, weights, turned_weights, turned_weights,
            pltpu.VMEM((exp_dev, units, slots // exp_dev), BF16),
            pltpu.VMEM((exp_dev, units, slots // exp_dev), BF16),
            weights, weights,
            dma((2,)),
            dma((2, exp_dev)),
            dma((CHUNKS,)),
            dma((CHUNKS,)),
            dma((CHUNKS,)),
            dma((CHUNKS,)),
            dma((2, CHUNKS)),
            dma((2, CHUNKS, len(ARRIVALS))),
            dma((2, CHUNKS)),
            dma((2, CHUNKS, RING, 2)),
            dma((2, CHUNKS, RING, 2)),
            dma((2, CHUNKS, RING - 1)),
        ],
        compiler_params=pltpu.CompilerParams(
            collective_id=0, has_side_effects=True, vmem_limit_bytes=60 * 1024 * 1024
        ),
        name="expert_layer",
    )(tokens.T, routes.T, gate_value.T, weight_in.transpose(0, 2, 1), weight_out, cotangent.T)
    layer_out, grad_tokens, grad_in, grad_out = pl.pallas_call(
        hand_over,
        out_shape=tuple(jax.ShapeDtypeStruct(out.shape, out.dtype) for out in outs),
        in_specs=[hbm] * len(outs),
        out_specs=(hbm,) * len(outs),
        scratch_shapes=[pltpu.VMEM(out.shape, out.dtype) for out in outs] + [dma((len(outs),)), dma((len(outs),))],
        compiler_params=pltpu.CompilerParams(vmem_limit_bytes=60 * 1024 * 1024),
        name="hand_over",
    )(*outs)
    return layer_out.T, grad_tokens.T, grad_in.transpose(0, 2, 1), grad_out


def solution(mesh):
    in_specs = (
        P("expert", "hidden"),
        P("expert", None),
        P("expert", None),
        P("expert", None, "hidden"),
        P("expert", "hidden", None),
        P("expert", "hidden"),
    )
    out_specs = (
        P("expert", "hidden"),
        P("expert", "hidden"),
        P("expert", None, "hidden"),
        P("expert", "hidden", None),
    )
    return jax.shard_map(local, mesh=mesh, in_specs=in_specs, out_specs=out_specs, check_vma=False)
```

```python
import functools

import jax
import jax.numpy as jnp
from jax import lax
from jax.experimental import pallas as pl
from jax.experimental.pallas import tpu as pltpu
from jax.sharding import PartitionSpec as P

MESH = pl.DeviceIdType.MESH
RING = 4
CORES = 2
CAP = 8
PAIR = 2
SIDES = 2
CHUNKS = 4
LANES = 128
F32 = jnp.float32
BF16 = jnp.bfloat16
NN = (((1,), (0,)), ((), ()))
NT = (((1,), (1,)), ((), ()))

PLACES = (0, -1, 1, 2)
ARRIVALS = [(-1, 0, None), (1, 0, None), (2, 0, None)]
for _i in PLACES:
    ARRIVALS += [(_i, -1, None), (_i, 1, None), (_i, 2, 0), (_i, 2, 1)]
ARRIVAL = {name: number for number, name in enumerate(ARRIVALS)}
ITEM = {2: 0, 1: 1, -1: 2, 0: 3}

ORDER = (
    ("S", 0), ("S", 1), ("F", 0, -1), ("F", 0, 1), ("R", 0, 0), ("F", 0, 2), ("F", 1, -1), ("F", 1, 1),
    ("S", 2), ("R", 1, 0), ("F", 1, 2), ("R", 0, -1), ("R", 0, 1), ("R", 0, 2), ("R", 1, -1), ("R", 1, 1),
    ("F", 2, -1), ("S", 3), ("F", 2, 1), ("R", 2, 0), ("F", 2, 2), ("R", 1, 2), ("R", 2, -1), ("F", 3, -1),
    ("F", 3, 1), ("R", 3, 0), ("F", 3, 2), ("R", 2, 1), ("R", 2, 2), ("C", 1, 0), ("C", 1, 1), ("R", 3, -1),
    ("R", 3, 1), ("R", 3, 2), ("C", 2, 0), ("C", 2, 1), ("M", 1, 2), ("M", 1, 1), ("M", 1, -1), ("M", 1, 0),
    ("C", 3, 0), ("C", 3, 1), ("M", 2, 2), ("M", 2, 1), ("M", 2, -1), ("M", 2, 0), ("U", 1, 2), ("U", 1, 1),
    ("U", 1, -1), ("C", 0, 0), ("C", 0, 1), ("M", 3, 1), ("M", 3, -1), ("M", 3, 2), ("M", 3, 0), ("U", 2, 2),
    ("U", 2, 1), ("U", 2, -1), ("Z", 1), ("M", 0, 2), ("M", 0, 1), ("M", 0, -1), ("M", 0, 0), ("U", 3, 1),
    ("U", 3, -1), ("U", 3, 2), ("Z", 2), ("U", 0, 2), ("U", 0, 1), ("U", 0, -1), ("Z", 3), ("Z", 0),
)
BACK = [_step[1] for _step in ORDER if _step[0] == "Z"]


def near(place):
    return (place + 1) % RING - 1


def dot(a, b, dims=NN):
    return lax.dot_general(a, b, dims, preferred_element_type=F32)


def gelu_and_slope(v):
    c = 0.7978845608028654
    square = v * v
    t = jnp.tanh(c * (v + 0.044715 * v * square))
    half = 0.5 * (1.0 + t)
    slope = half + 0.5 * v * (1.0 - t * t) * (c + c * 3.0 * 0.044715 * square)
    return v * half, slope


def kernel(
    tokens_hbm, routes_hbm, gate_hbm, wint_ref, wout_ref, cot_hbm,
    layer_ref, gtok_ref, gwint_ref, gwout_ref,
    tokens_ref, routes_ref, gate_ref, cot_ref, chosen_v, send_v, recv_v, bsend_v, back_v, xg_v, part_v, via_v, frm_v, last_v,
    wint_v, wout_v, win_v, woutt_v, hid_v, gp_v, gwint_v, gwout_v,
    in_sem, w_sem, gw_sem, a2a_send, a2a_recv, back_send, back_recv,
    ag_send, ag_recv, rs_send, via_recv, frm_recv, last_recv,
):
    owners = lax.axis_size("expert")
    feat, tok = tokens_hbm.shape
    exp_dev, units, width = wint_ref.shape
    rows = PAIR * CAP
    length = owners // SIDES * rows
    half = length // PAIR
    chips = owners // CORES
    side_chips = chips // SIDES
    pairs = exp_dev // PAIR
    behind = max(side_chips // 2 - 1, 0)
    me = lax.axis_index("expert")
    here = lax.axis_index("hidden")
    chip, core = me // CORES, lax.rem(me, CORES)
    x, y = here // RING, lax.rem(here, RING)

    def hidden_at(dx, dy):
        return lax.rem(x + dx + RING, RING) * RING + lax.rem(y + dy + RING, RING)

    def place(part, i, j):
        return hidden_at(i, j) if part == 0 else hidden_at(j, i)

    def neighbour(part, axis, step):
        return (me, place(part, step, 0) if axis == 0 else place(part, 0, step))

    barrier = pltpu.get_barrier_semaphore()

    def greet(i, carry):
        offset = owners // 2 + jnp.where(lax.rem(i, 2) == 1, (i + 1) // 2, -((i + 1) // 2))
        pl.semaphore_signal(barrier, inc=1, device_id=(lax.rem(me + offset, owners), here), device_id_type=MESH)
        return carry

    lax.fori_loop(0, owners - 1, greet, 0)
    inputs = [
        pltpu.make_async_copy(src, dst, in_sem.at[number])
        for number, (src, dst) in enumerate(
            ((routes_hbm, routes_ref), (tokens_hbm, tokens_ref), (cot_hbm, cot_ref), (gate_hbm, gate_ref))
        )
    ]
    for copy in inputs:
        copy.start()
    for step in (1, -1, 2):
        for axis in (0, 1):
            pl.semaphore_signal(barrier, inc=1, device_id=neighbour(0, axis, step), device_id_type=MESH)
    wint_copy = pltpu.make_async_copy(wint_ref, wint_v, w_sem.at[0])
    wout_copy = pltpu.make_async_copy(wout_ref, wout_v, w_sem.at[1])
    wint_copy.start()
    wout_copy.start()
    for copy in inputs:
        copy.wait()

    routes = routes_ref[...]
    experts = owners * exp_dev
    matches = jnp.where(routes == lax.broadcasted_iota(jnp.int32, (experts, tok), 0), 1.0, 0.0)
    earlier = jnp.where(
        lax.broadcasted_iota(jnp.int32, (tok, tok), 0) < lax.broadcasted_iota(jnp.int32, (tok, tok), 1), 1.0, 0.0
    ).astype(BF16)
    before = dot(matches.astype(BF16), earlier)
    slot = jnp.sum(before * matches, axis=0, keepdims=True).astype(jnp.int32)
    owner = routes // exp_dev
    pair_at = (routes & (exp_dev - 1)) // PAIR
    number_at = (chip - owner // CORES + behind + chips) & (chips - 1)
    block_at = ((number_at // side_chips * pairs + pair_at) * side_chips + (number_at & (side_chips - 1))) * CORES
    pos = (block_at + (owner & (CORES - 1))) * rows + (routes & (PAIR - 1)) * CAP + slot
    scaled = gate_ref[...] * cot_ref[...].astype(F32)
    empty = jnp.zeros((LANES - 2 * feat, tok), BF16)
    both = jnp.concatenate([tokens_ref[...], scaled.astype(BF16), empty], axis=0)
    chosen_v[...] = jnp.where(
        lax.broadcasted_iota(jnp.int32, chosen_v.shape, 0) == pos, 1.0, 0.0
    ).astype(BF16)
    send_v[...] = dot(chosen_v[...], both, NT).astype(BF16)

    pl.semaphore_wait(barrier, owners - 1 + 6)

    def block(number):
        return pl.ds(pl.multiple_of(number * rows, rows), rows)

    def exchange(c, outward, src, dst, send_sem, recv_sem):
        side = c // pairs
        for number in sorted(
            range(side_chips), key=lambda k: -min((side * side_chips + k - behind) % chips, (behind - side * side_chips - k) % chips)
        ):
            ahead = side * side_chips + number - behind
            way = -ahead if outward else ahead
            for other in range(CORES):
                to_core = lax.rem(core + other, CORES)
                to = lax.rem(chip + way + chips, chips) * CORES + to_core
                take = (c * side_chips + number) * CORES + to_core
                put = (c * side_chips + number) * CORES + core
                if ahead == 0 and other == 0:
                    dst[block(put), :] = src[block(take), :]
                else:
                    pltpu.make_async_remote_copy(
                        src_ref=src.at[block(take)], dst_ref=dst.at[block(put)],
                        send_sem=send_sem.at[c], recv_sem=recv_sem.at[c], device_id=(to, here), device_id_type=MESH,
                    ).start()

    def exchange_wait(c, ref, sem):
        view = ref.at[pl.ds(0, length - rows if c // pairs == 0 else length)]
        pltpu.make_async_copy(view, view, sem.at[c]).wait()

    for c in range(CHUNKS):
        exchange(c, True, send_v, recv_v, a2a_send, a2a_recv)

    wint_copy.wait()
    wout_copy.wait()
    for e in range(exp_dev):
        win_v[e] = jnp.transpose(wint_v[e])
        woutt_v[e] = jnp.transpose(wout_v[e])

    def lanes_of(ref, which):
        return ref if which is None else ref.at[:, pl.ds(which * half, half)]

    def ag_copy(part, p, i, j, which, axis, step):
        ref = lanes_of(xg_v.at[part, p, place(part, i, j)], which)
        there = (near(i - step), j, which) if axis == 0 else (i, near(j - step), which)
        return pltpu.make_async_remote_copy(
            src_ref=ref, dst_ref=ref, send_sem=ag_send.at[part, p],
            recv_sem=ag_recv.at[part, p, ARRIVAL[there]],
            device_id=neighbour(part, axis, step), device_id_type=MESH,
        )

    def ag_send_to(part, p, i, j, which, axis, step):
        ag_copy(part, p, i, j, which, axis, step).start()

    def ag_wait(part, p, i, j, which=None):
        ref = lanes_of(xg_v.at[part, p, place(part, i, j)], which)
        pltpu.make_async_copy(ref, ref, ag_recv.at[part, p, ARRIVAL[(i, j, which)]]).wait()

    def ag_start(p):
        exchange_wait(p, recv_v, a2a_recv)
        arrived = recv_v[p * length:(p + 1) * length].astype(F32).reshape(length // rows, PAIR, CAP, LANES)
        for e in range(PAIR):
            turned = jnp.transpose(arrived[:, e].reshape(half, LANES))
            for part in range(2):
                xg_v[part, p, here, :, e * half:(e + 1) * half] = turned[part * feat:(part + 1) * feat].astype(BF16)
        for axis, step in ((0, 1), (0, -1), (0, 2), (1, 1), (1, -1)):
            for part in range(2):
                ag_send_to(part, p, 0, 0, None, axis, step)

    def ag_column(p, i):
        for part in range(2):
            ag_wait(part, p, i, 0)
            for step in (1, -1):
                ag_send_to(part, p, i, 0, None, 1, step)

    def ag_row(p, i):
        for which, step in ((0, 1), (1, -1)):
            for part in range(2):
                ag_wait(part, p, i, -step)
                ag_send_to(part, p, i, -step, which, 1, step)

    def ag_end(p):
        for i in PLACES:
            for part in range(2):
                for which in range(2):
                    ag_wait(part, p, i, 2, which)

    def rows_of(part, p, which):
        return xg_v[part, p, :, :, which * half:(which + 1) * half].reshape(width, half)

    def forward_backward(p, which):
        side, e = p // pairs, p % pairs * PAIR + which
        at, own = slice(which * half, (which + 1) * half), slice(side * half, (side + 1) * half)
        act, slope = gelu_and_slope(dot(wint_v[e], rows_of(0, p, which)))
        act = act.astype(BF16)
        hid_v[e, :, own] = act
        part_v[0, p, :, :, at] = dot(woutt_v[e], act).astype(BF16).reshape(width // feat, feat, half)
        grad = (dot(wout_v[e], rows_of(1, p, which)) * slope).astype(BF16)
        gp_v[e, :, own] = grad
        part_v[1, p, :, :, at] = dot(win_v[e], grad).astype(BF16).reshape(width // feat, feat, half)

    def weight_grads(e):
        rows_x, rows_g = [
            jnp.concatenate([rows_of(part, side * pairs + e // PAIR, e % PAIR) for side in range(SIDES)], axis=1)
            for part in range(2)
        ]
        gwint_v[e] = dot(gp_v[e], rows_x, NT).astype(BF16)
        pltpu.make_async_copy(gwint_v.at[e], gwint_ref.at[e], gw_sem.at[0, e]).start()
        gwout_v[e] = dot(hid_v[e], rows_g, NT).astype(BF16)
        pltpu.make_async_copy(gwout_v.at[e], gwout_ref.at[e], gw_sem.at[1, e]).start()

    def rs_copy(part, p, i, j, which, axis, step, dst, sem):
        pltpu.make_async_remote_copy(
            src_ref=lanes_of(part_v.at[part, p, place(part, i, j)], which), dst_ref=dst,
            send_sem=rs_send.at[part, p], recv_sem=sem,
            device_id=neighbour(part, axis, step), device_id_type=MESH,
        ).start()

    def rs_through(part, p, i, which, step):
        rs_copy(part, p, i, 2, which, 1, step, via_v.at[part, p, ITEM[i], which], via_recv.at[part, p, ITEM[i], which])

    def rs_to(part, p, i, which, step):
        number = 0 if step == 1 else 1
        dst = lanes_of(frm_v.at[part, p, ITEM[i], number], which)
        rs_copy(part, p, i, step, which, 1, step, dst, frm_recv.at[part, p, ITEM[i], number])

    def rs_start(p, which):
        step = 1 if which == 0 else -1
        for i in ITEM:
            for part in range(2):
                rs_through(part, p, i, which, step)
        for i in ITEM:
            for part in range(2):
                rs_to(part, p, i, which, -step)

    def rs_middle(p, i):
        for which, step in ((0, 1), (1, -1)):
            for part in range(2):
                buf, sem = via_v.at[part, p, ITEM[i], which], via_recv.at[part, p, ITEM[i], which]
                pltpu.make_async_copy(buf, buf, sem).wait()
                ref = lanes_of(part_v.at[part, p, place(part, i, step)], which)
                ref[...] = (ref[...].astype(F32) + buf[...].astype(F32)).astype(BF16)
                rs_to(part, p, i, which, step)

    def rs_total(part, p, i):
        total = part_v[part, p, place(part, i, 0)].astype(F32)
        for number in range(2):
            buf = frm_v.at[part, p, ITEM[i], number]
            pltpu.make_async_copy(buf, buf, frm_recv.at[part, p, ITEM[i], number]).wait()
            total = total + buf[...].astype(F32)
        return total

    def rs_sum(p, i):
        for part in range(2):
            part_v[part, p, place(part, i, 0)] = rs_total(part, p, i).astype(BF16)
            rs_copy(part, p, i, 0, None, 0, i, last_v.at[part, p, ITEM[i]], last_recv.at[part, p, ITEM[i]])

    def rs_last(part, p):
        total = rs_total(part, p, 0)
        for i in (1, -1, 2):
            buf = last_v.at[part, p, ITEM[i]]
            pltpu.make_async_copy(buf, buf, last_recv.at[part, p, ITEM[i]]).wait()
            total = total + buf[...].astype(F32)
        return total.astype(BF16).astype(F32)

    def rs_end(p):
        totals = [rs_last(part, p) for part in range(2)]
        totals.append(jnp.zeros((LANES - 2 * feat, length), F32))
        turned = jnp.transpose(jnp.concatenate(totals, axis=0)).reshape(PAIR, length // rows, CAP, LANES)
        turned = jnp.concatenate([turned[e][:, None] for e in range(PAIR)], axis=1)
        bsend_v[p * length:(p + 1) * length] = turned.reshape(length, LANES).astype(BF16)
        exchange(p, False, bsend_v, back_v, back_send, back_recv)

    def compute(p, which):
        if which == 0:
            ag_end(p)
        forward_backward(p, which)
        rs_start(p, which)

    for step, *on in ORDER:
        {"S": ag_start, "F": ag_column, "R": ag_row, "C": compute, "M": rs_middle, "U": rs_sum, "Z": rs_end}[step](*on)
    for e in range(exp_dev):
        weight_grads(e)

    taken = jnp.zeros((LANES, tok), F32)
    for p in BACK:
        exchange_wait(p, back_v, back_recv)
        at = slice(p * length, (p + 1) * length)
        turned = jnp.transpose(back_v[at].astype(F32)).astype(BF16)
        taken = taken + dot(turned, chosen_v[at])
    layer_ref[...] = (gate_ref[...] * taken[0:feat]).astype(BF16)
    gtok_ref[...] = taken[feat:2 * feat].astype(BF16)

    for expert in range(exp_dev):
        pltpu.make_async_copy(gwint_v.at[expert], gwint_ref.at[expert], gw_sem.at[0, expert]).wait()
        pltpu.make_async_copy(gwout_v.at[expert], gwout_ref.at[expert], gw_sem.at[1, expert]).wait()
    for p in range(CHUNKS):
        exchange_wait(p, send_v, a2a_send)
        exchange_wait(p, bsend_v, back_send)
        for part in range(2):
            for buf, sem in ((xg_v, ag_send), (part_v, rs_send)):
                view = buf.at[part, p, pl.ds(0, RING * RING - 1)]
                pltpu.make_async_copy(view, view, sem.at[part, p]).wait()


def hand_over(*refs):
    count = (len(refs) - 2) // 3
    in_sem, out_sem = refs[3 * count:]
    pieces = []
    for i in range(count):
        three = [refs[i + k * count] for k in range(3)]
        if len(three[0].shape) == 3:
            pieces += [[ref.at[e] for ref in three] for e in range(three[0].shape[0])]
        else:
            pieces.append(three)
    into = [pltpu.make_async_copy(given, held, in_sem.at[i]) for i, (given, out, held) in enumerate(pieces)]
    away = [pltpu.make_async_copy(held, out, out_sem.at[i]) for i, (given, out, held) in enumerate(pieces)]
    for copy in into:
        copy.start()
    for first, second in zip(into, away):
        first.wait()
        second.start()
    for copy in away:
        copy.wait()


def local(tokens, routes, gate_value, weight_in, weight_out, cotangent):
    owners = lax.axis_size("expert")
    blocks = lax.axis_size("hidden")
    tok, feat = tokens.shape
    exp_dev, width, units = weight_in.shape
    slots = owners * exp_dev * CAP
    length = owners // SIDES * PAIR * CAP
    half = length // PAIR
    vmem = pl.BlockSpec(memory_space=pltpu.VMEM)
    hbm = pl.BlockSpec(memory_space=pl.ANY)
    dma = pltpu.SemaphoreType.DMA
    weights = pltpu.VMEM((exp_dev, units, width), BF16)
    turned_weights = pltpu.VMEM((exp_dev, width, units), BF16)
    rows = pltpu.VMEM((slots, LANES), BF16)
    outs = pl.pallas_call(
        kernel,
        out_shape=(
            jax.ShapeDtypeStruct((feat, tok), BF16),
            jax.ShapeDtypeStruct((feat, tok), BF16),
            jax.ShapeDtypeStruct((exp_dev, units, width), BF16),
            jax.ShapeDtypeStruct((exp_dev, units, width), BF16),
        ),
        in_specs=[hbm] * 6,
        out_specs=(vmem, vmem, hbm, hbm),
        scratch_shapes=[
            pltpu.VMEM((feat, tok), BF16),
            pltpu.VMEM((1, tok), jnp.int32),
            pltpu.VMEM((1, tok), F32),
            pltpu.VMEM((feat, tok), BF16),
            pltpu.VMEM((slots, tok), BF16),
            rows, rows, rows, rows,
            pltpu.VMEM((2, CHUNKS, blocks, feat, length), BF16),
            pltpu.VMEM((2, CHUNKS, blocks, feat, length), BF16),
            pltpu.VMEM((2, CHUNKS, RING, 2, feat, half), BF16),
            pltpu.VMEM((2, CHUNKS, RING, 2, feat, length), BF16),
            pltpu.VMEM((2, CHUNKS, RING - 1, feat, length), BF16),
            weights, weights, turned_weights, turned_weights,
            pltpu.VMEM((exp_dev, units, slots // exp_dev), BF16),
            pltpu.VMEM((exp_dev, units, slots // exp_dev), BF16),
            weights, weights,
            dma((4,)),
            dma((2,)),
            dma((2, exp_dev)),
            dma((CHUNKS,)),
            dma((CHUNKS,)),
            dma((CHUNKS,)),
            dma((CHUNKS,)),
            dma((2, CHUNKS)),
            dma((2, CHUNKS, len(ARRIVALS))),
            dma((2, CHUNKS)),
            dma((2, CHUNKS, RING, 2)),
            dma((2, CHUNKS, RING, 2)),
            dma((2, CHUNKS, RING - 1)),
        ],
        compiler_params=pltpu.CompilerParams(
            collective_id=0, has_side_effects=True, vmem_limit_bytes=60 * 1024 * 1024
        ),
        name="expert_layer",
    )(tokens.T, routes.T, gate_value.T, weight_in.transpose(0, 2, 1), weight_out, cotangent.T)
    layer_out, grad_tokens, grad_in, grad_out = pl.pallas_call(
        hand_over,
        out_shape=tuple(jax.ShapeDtypeStruct(out.shape, out.dtype) for out in outs),
        in_specs=[hbm] * len(outs),
        out_specs=(hbm,) * len(outs),
        scratch_shapes=[pltpu.VMEM(out.shape, out.dtype) for out in outs] + [dma((2 + 2 * exp_dev,)), dma((2 + 2 * exp_dev,))],
        compiler_params=pltpu.CompilerParams(vmem_limit_bytes=60 * 1024 * 1024),
        name="hand_over",
    )(*outs)
    return layer_out.T, grad_tokens.T, grad_in.transpose(0, 2, 1), grad_out


def solution(mesh):
    in_specs = (
        P("expert", "hidden"),
        P("expert", None),
        P("expert", None),
        P("expert", None, "hidden"),
        P("expert", "hidden", None),
        P("expert", "hidden"),
    )
    out_specs = (
        P("expert", "hidden"),
        P("expert", "hidden"),
        P("expert", None, "hidden"),
        P("expert", "hidden", None),
    )
    return jax.shard_map(local, mesh=mesh, in_specs=in_specs, out_specs=out_specs, check_vma=False)
```

```python
import functools

import jax
import jax.numpy as jnp
from jax import lax
from jax.experimental import pallas as pl
from jax.experimental.pallas import tpu as pltpu
from jax.sharding import PartitionSpec as P

MESH = pl.DeviceIdType.MESH
RING = 4
CORES = 2
CAP = 8
PAIR = 2
SIDES = 2
CHUNKS = 4
LANES = 128
F32 = jnp.float32
BF16 = jnp.bfloat16
NN = (((1,), (0,)), ((), ()))
NT = (((1,), (1,)), ((), ()))

PLACES = (0, -1, 1, 2)
ARRIVALS = [(-1, 0, None), (1, 0, None), (2, 0, None)]
for _i in PLACES:
    ARRIVALS += [(_i, -1, None), (_i, 1, None), (_i, 2, 0), (_i, 2, 1)]
ARRIVAL = {name: number for number, name in enumerate(ARRIVALS)}
ITEM = {2: 0, 1: 1, -1: 2, 0: 3}

ORDER = (
    ("S", 0), ("F", 0, -1), ("F", 0, 1), ("R", 0, 0), ("F", 0, 2), ("S", 2), ("R", 0, -1), ("R", 0, 1),
    ("R", 0, 2), ("F", 2, -1), ("F", 2, 1), ("S", 3), ("R", 2, 0), ("F", 2, 2), ("S", 1), ("R", 2, -1),
    ("R", 2, 1), ("F", 3, -1), ("F", 3, 1), ("R", 3, 0), ("F", 3, 2), ("R", 2, 2), ("F", 1, -1), ("F", 1, 1),
    ("R", 1, 0), ("F", 1, 2), ("R", 3, -1), ("R", 3, 1), ("R", 3, 2), ("C", 2, 0), ("C", 2, 1), ("R", 1, -1),
    ("R", 1, 1), ("R", 1, 2), ("C", 3, 0), ("C", 3, 1), ("M", 2, 2), ("M", 2, 1), ("M", 2, -1), ("M", 2, 0),
    ("C", 1, 0), ("C", 1, 1), ("M", 3, 2), ("M", 3, 1), ("M", 3, -1), ("M", 3, 0), ("U", 2, 2), ("U", 2, 1),
    ("U", 2, -1), ("C", 0, 0), ("C", 0, 1), ("M", 1, 2), ("M", 1, 1), ("M", 1, -1), ("M", 1, 0), ("U", 3, 2),
    ("U", 3, 1), ("U", 3, -1), ("Z", 2), ("M", 0, 2), ("M", 0, 1), ("M", 0, -1), ("M", 0, 0), ("U", 1, 2),
    ("U", 1, 1), ("U", 1, -1), ("Z", 3), ("U", 0, 2), ("U", 0, 1), ("U", 0, -1), ("Z", 1), ("Z", 0),
)
BACK = [_step[1] for _step in ORDER if _step[0] == "Z"]


def near(place):
    return (place + 1) % RING - 1


def dot(a, b, dims=NN):
    return lax.dot_general(a, b, dims, preferred_element_type=F32)


def gelu_and_slope(v):
    c = 0.7978845608028654
    square = v * v
    t = jnp.tanh(c * (v + 0.044715 * v * square))
    half = 0.5 * (1.0 + t)
    slope = half + 0.5 * v * (1.0 - t * t) * (c + c * 3.0 * 0.044715 * square)
    return v * half, slope


def kernel(
    tokens_hbm, routes_hbm, gate_hbm, wint_ref, wout_ref, cot_hbm,
    layer_ref, gtok_ref, gwint_ref, gwout_ref,
    tokens_ref, routes_ref, gate_ref, cot_ref, chosen_v, send_v, recv_v, bsend_v, back_v, xg_v, part_v, via_v, frm_v, last_v,
    wint_v, wout_v, win_v, woutt_v, hid_v, gp_v, gwint_v, gwout_v,
    in_sem, w_sem, gw_sem, a2a_send, a2a_recv, back_send, back_recv,
    ag_send, ag_recv, rs_send, via_recv, frm_recv, last_recv,
):
    owners = lax.axis_size("expert")
    feat, tok = tokens_hbm.shape
    exp_dev, units, width = wint_ref.shape
    rows = PAIR * CAP
    length = owners // SIDES * rows
    half = length // PAIR
    chips = owners // CORES
    side_chips = chips // SIDES
    pairs = exp_dev // PAIR
    behind = max(side_chips // 2 - 1, 0)
    me = lax.axis_index("expert")
    here = lax.axis_index("hidden")
    chip, core = me // CORES, lax.rem(me, CORES)
    x, y = here // RING, lax.rem(here, RING)

    def hidden_at(dx, dy):
        return lax.rem(x + dx + RING, RING) * RING + lax.rem(y + dy + RING, RING)

    def place(part, i, j):
        return hidden_at(i, j) if part == 0 else hidden_at(j, i)

    def neighbour(part, axis, step):
        return (me, place(part, step, 0) if axis == 0 else place(part, 0, step))

    barrier = pltpu.get_barrier_semaphore()

    def greet(i, carry):
        offset = owners // 2 + jnp.where(lax.rem(i, 2) == 1, (i + 1) // 2, -((i + 1) // 2))
        pl.semaphore_signal(barrier, inc=1, device_id=(lax.rem(me + offset, owners), here), device_id_type=MESH)
        return carry

    lax.fori_loop(0, owners - 1, greet, 0)
    inputs = [
        pltpu.make_async_copy(src, dst, in_sem.at[number])
        for number, (src, dst) in enumerate(
            ((routes_hbm, routes_ref), (tokens_hbm, tokens_ref), (cot_hbm, cot_ref), (gate_hbm, gate_ref))
        )
    ]
    for copy in inputs:
        copy.start()
    for step in (1, -1, 2):
        for axis in (0, 1):
            pl.semaphore_signal(barrier, inc=1, device_id=neighbour(0, axis, step), device_id_type=MESH)
    wint_copy = pltpu.make_async_copy(wint_ref, wint_v, w_sem.at[0])
    wout_copy = pltpu.make_async_copy(wout_ref, wout_v, w_sem.at[1])
    wint_copy.start()
    wout_copy.start()
    for copy in inputs:
        copy.wait()

    routes = routes_ref[...]
    experts = owners * exp_dev
    matches = jnp.where(routes == lax.broadcasted_iota(jnp.int32, (experts, tok), 0), 1.0, 0.0)
    earlier = jnp.where(
        lax.broadcasted_iota(jnp.int32, (tok, tok), 0) < lax.broadcasted_iota(jnp.int32, (tok, tok), 1), 1.0, 0.0
    ).astype(BF16)
    before = dot(matches.astype(BF16), earlier)
    slot = jnp.sum(before * matches, axis=0, keepdims=True).astype(jnp.int32)
    owner = routes // exp_dev
    pair_at = (routes & (exp_dev - 1)) // PAIR
    number_at = (chip - owner // CORES + behind + chips) & (chips - 1)
    block_at = ((number_at // side_chips * pairs + pair_at) * side_chips + (number_at & (side_chips - 1))) * CORES
    pos = (block_at + (owner & (CORES - 1))) * rows + (routes & (PAIR - 1)) * CAP + slot
    scaled = gate_ref[...] * cot_ref[...].astype(F32)
    empty = jnp.zeros((LANES - 2 * feat, tok), BF16)
    both = jnp.concatenate([tokens_ref[...], scaled.astype(BF16), empty], axis=0)
    chosen_v[...] = jnp.where(
        lax.broadcasted_iota(jnp.int32, chosen_v.shape, 0) == pos, 1.0, 0.0
    ).astype(BF16)
    send_v[...] = dot(chosen_v[...], both, NT).astype(BF16)

    pl.semaphore_wait(barrier, owners - 1 + 6)

    def block(number):
        return pl.ds(pl.multiple_of(number * rows, rows), rows)

    def exchange(c, outward, src, dst, send_sem, recv_sem):
        side = c // pairs
        for number in sorted(
            range(side_chips), key=lambda k: -min((side * side_chips + k - behind) % chips, (behind - side * side_chips - k) % chips)
        ):
            ahead = side * side_chips + number - behind
            way = -ahead if outward else ahead
            for other in range(CORES):
                to_core = lax.rem(core + other, CORES)
                to = lax.rem(chip + way + chips, chips) * CORES + to_core
                take = (c * side_chips + number) * CORES + to_core
                put = (c * side_chips + number) * CORES + core
                if ahead == 0 and other == 0:
                    dst[block(put), :] = src[block(take), :]
                else:
                    pltpu.make_async_remote_copy(
                        src_ref=src.at[block(take)], dst_ref=dst.at[block(put)],
                        send_sem=send_sem.at[c], recv_sem=recv_sem.at[c], device_id=(to, here), device_id_type=MESH,
                    ).start()

    def exchange_wait(c, ref, sem):
        view = ref.at[pl.ds(0, length - rows if c // pairs == 0 else length)]
        pltpu.make_async_copy(view, view, sem.at[c]).wait()

    for c in range(CHUNKS):
        exchange(c, True, send_v, recv_v, a2a_send, a2a_recv)

    wint_copy.wait()
    wout_copy.wait()
    for e in range(exp_dev):
        win_v[e] = jnp.transpose(wint_v[e])
        woutt_v[e] = jnp.transpose(wout_v[e])

    def lanes_of(ref, which):
        return ref if which is None else ref.at[:, pl.ds(which * half, half)]

    def ag_copy(part, p, i, j, which, axis, step):
        ref = lanes_of(xg_v.at[part, p, place(part, i, j)], which)
        there = (near(i - step), j, which) if axis == 0 else (i, near(j - step), which)
        return pltpu.make_async_remote_copy(
            src_ref=ref, dst_ref=ref, send_sem=ag_send.at[part, p],
            recv_sem=ag_recv.at[part, p, ARRIVAL[there]],
            device_id=neighbour(part, axis, step), device_id_type=MESH,
        )

    def ag_send_to(part, p, i, j, which, axis, step):
        ag_copy(part, p, i, j, which, axis, step).start()

    def ag_wait(part, p, i, j, which=None):
        ref = lanes_of(xg_v.at[part, p, place(part, i, j)], which)
        pltpu.make_async_copy(ref, ref, ag_recv.at[part, p, ARRIVAL[(i, j, which)]]).wait()

    def ag_start(p):
        exchange_wait(p, recv_v, a2a_recv)
        arrived = recv_v[p * length:(p + 1) * length].astype(F32).reshape(length // rows, PAIR, CAP, LANES)
        for e in range(PAIR):
            turned = jnp.transpose(arrived[:, e].reshape(half, LANES))
            for part in range(2):
                xg_v[part, p, here, :, e * half:(e + 1) * half] = turned[part * feat:(part + 1) * feat].astype(BF16)
        for axis, step in ((0, 2), (0, 1), (0, -1), (1, 1), (1, -1)):
            for part in range(2):
                ag_send_to(part, p, 0, 0, None, axis, step)

    def ag_column(p, i):
        for part in range(2):
            ag_wait(part, p, i, 0)
            for step in (1, -1):
                ag_send_to(part, p, i, 0, None, 1, step)

    def ag_row(p, i):
        for which, step in ((0, 1), (1, -1)):
            for part in range(2):
                ag_wait(part, p, i, -step)
                ag_send_to(part, p, i, -step, which, 1, step)

    def ag_end(p):
        for i in PLACES:
            for part in range(2):
                for which in range(2):
                    ag_wait(part, p, i, 2, which)

    def rows_of(part, p, which):
        return xg_v[part, p, :, :, which * half:(which + 1) * half].reshape(width, half)

    def forward_backward(p, which):
        side, e = p // pairs, p % pairs * PAIR + which
        at, own = slice(which * half, (which + 1) * half), slice(side * half, (side + 1) * half)
        act, slope = gelu_and_slope(dot(wint_v[e], rows_of(0, p, which)))
        act = act.astype(BF16)
        hid_v[e, :, own] = act
        part_v[0, p, :, :, at] = dot(woutt_v[e], act).astype(BF16).reshape(width // feat, feat, half)
        grad = (dot(wout_v[e], rows_of(1, p, which)) * slope).astype(BF16)
        gp_v[e, :, own] = grad
        part_v[1, p, :, :, at] = dot(win_v[e], grad).astype(BF16).reshape(width // feat, feat, half)

    def weight_grads(e):
        rows_x, rows_g = [
            jnp.concatenate([rows_of(part, side * pairs + e // PAIR, e % PAIR) for side in range(SIDES)], axis=1)
            for part in range(2)
        ]
        gwint_v[e] = dot(gp_v[e], rows_x, NT).astype(BF16)
        pltpu.make_async_copy(gwint_v.at[e], gwint_ref.at[e], gw_sem.at[0, e]).start()
        gwout_v[e] = dot(hid_v[e], rows_g, NT).astype(BF16)
        pltpu.make_async_copy(gwout_v.at[e], gwout_ref.at[e], gw_sem.at[1, e]).start()

    def rs_copy(part, p, i, j, which, axis, step, dst, sem):
        pltpu.make_async_remote_copy(
            src_ref=lanes_of(part_v.at[part, p, place(part, i, j)], which), dst_ref=dst,
            send_sem=rs_send.at[part, p], recv_sem=sem,
            device_id=neighbour(part, axis, step), device_id_type=MESH,
        ).start()

    def rs_through(part, p, i, which, step):
        rs_copy(part, p, i, 2, which, 1, step, via_v.at[part, p, ITEM[i], which], via_recv.at[part, p, ITEM[i], which])

    def rs_to(part, p, i, which, step):
        number = 0 if step == 1 else 1
        dst = lanes_of(frm_v.at[part, p, ITEM[i], number], which)
        rs_copy(part, p, i, step, which, 1, step, dst, frm_recv.at[part, p, ITEM[i], number])

    def rs_start(p, which):
        step = 1 if which == 0 else -1
        for i in ITEM:
            for part in range(2):
                rs_through(part, p, i, which, step)
        for i in ITEM:
            for part in range(2):
                rs_to(part, p, i, which, -step)

    def rs_middle(p, i):
        for which, step in ((0, 1), (1, -1)):
            for part in range(2):
                buf, sem = via_v.at[part, p, ITEM[i], which], via_recv.at[part, p, ITEM[i], which]
                pltpu.make_async_copy(buf, buf, sem).wait()
                ref = lanes_of(part_v.at[part, p, place(part, i, step)], which)
                ref[...] = (ref[...].astype(F32) + buf[...].astype(F32)).astype(BF16)
                rs_to(part, p, i, which, step)

    def rs_total(part, p, i):
        total = part_v[part, p, place(part, i, 0)].astype(F32)
        for number in range(2):
            buf = frm_v.at[part, p, ITEM[i], number]
            pltpu.make_async_copy(buf, buf, frm_recv.at[part, p, ITEM[i], number]).wait()
            total = total + buf[...].astype(F32)
        return total

    def rs_sum(p, i):
        for part in range(2):
            part_v[part, p, place(part, i, 0)] = rs_total(part, p, i).astype(BF16)
            rs_copy(part, p, i, 0, None, 0, i, last_v.at[part, p, ITEM[i]], last_recv.at[part, p, ITEM[i]])

    def rs_last(part, p):
        total = rs_total(part, p, 0)
        for i in (1, -1, 2):
            buf = last_v.at[part, p, ITEM[i]]
            pltpu.make_async_copy(buf, buf, last_recv.at[part, p, ITEM[i]]).wait()
            total = total + buf[...].astype(F32)
        return total.astype(BF16).astype(F32)

    def rs_end(p):
        totals = [rs_last(part, p) for part in range(2)]
        totals.append(jnp.zeros((LANES - 2 * feat, length), F32))
        turned = jnp.transpose(jnp.concatenate(totals, axis=0)).reshape(PAIR, length // rows, CAP, LANES)
        turned = jnp.concatenate([turned[e][:, None] for e in range(PAIR)], axis=1)
        bsend_v[p * length:(p + 1) * length] = turned.reshape(length, LANES).astype(BF16)
        exchange(p, False, bsend_v, back_v, back_send, back_recv)

    def compute(p, which):
        if which == 0:
            ag_end(p)
        forward_backward(p, which)
        rs_start(p, which)

    for step, *on in ORDER:
        {"S": ag_start, "F": ag_column, "R": ag_row, "C": compute, "M": rs_middle, "U": rs_sum, "Z": rs_end}[step](*on)
    for e in range(exp_dev):
        weight_grads(e)

    taken = jnp.zeros((LANES, tok), F32)
    for p in BACK:
        exchange_wait(p, back_v, back_recv)
        at = slice(p * length, (p + 1) * length)
        turned = jnp.transpose(back_v[at].astype(F32)).astype(BF16)
        taken = taken + dot(turned, chosen_v[at])
    layer_ref[...] = (gate_ref[...] * taken[0:feat]).astype(BF16)
    gtok_ref[...] = taken[feat:2 * feat].astype(BF16)

    for expert in range(exp_dev):
        pltpu.make_async_copy(gwint_v.at[expert], gwint_ref.at[expert], gw_sem.at[0, expert]).wait()
        pltpu.make_async_copy(gwout_v.at[expert], gwout_ref.at[expert], gw_sem.at[1, expert]).wait()
    for p in range(CHUNKS):
        exchange_wait(p, send_v, a2a_send)
        exchange_wait(p, bsend_v, back_send)
        for part in range(2):
            for buf, sem in ((xg_v, ag_send), (part_v, rs_send)):
                view = buf.at[part, p, pl.ds(0, RING * RING - 1)]
                pltpu.make_async_copy(view, view, sem.at[part, p]).wait()


def hand_over(*refs):
    count = (len(refs) - 2) // 3
    in_sem, out_sem = refs[3 * count:]
    pieces = []
    for i in range(count):
        three = [refs[i + k * count] for k in range(3)]
        if len(three[0].shape) == 3:
            pieces += [[ref.at[e] for ref in three] for e in range(three[0].shape[0])]
        else:
            pieces.append(three)
    into = [pltpu.make_async_copy(given, held, in_sem.at[i]) for i, (given, out, held) in enumerate(pieces)]
    away = [pltpu.make_async_copy(held, out, out_sem.at[i]) for i, (given, out, held) in enumerate(pieces)]
    for copy in into:
        copy.start()
    for first, second in zip(into, away):
        first.wait()
        second.start()
    for copy in away:
        copy.wait()


def local(tokens, routes, gate_value, weight_in, weight_out, cotangent):
    owners = lax.axis_size("expert")
    blocks = lax.axis_size("hidden")
    tok, feat = tokens.shape
    exp_dev, width, units = weight_in.shape
    slots = owners * exp_dev * CAP
    length = owners // SIDES * PAIR * CAP
    half = length // PAIR
    vmem = pl.BlockSpec(memory_space=pltpu.VMEM)
    hbm = pl.BlockSpec(memory_space=pl.ANY)
    dma = pltpu.SemaphoreType.DMA
    weights = pltpu.VMEM((exp_dev, units, width), BF16)
    turned_weights = pltpu.VMEM((exp_dev, width, units), BF16)
    rows = pltpu.VMEM((slots, LANES), BF16)
    outs = pl.pallas_call(
        kernel,
        out_shape=(
            jax.ShapeDtypeStruct((feat, tok), BF16),
            jax.ShapeDtypeStruct((feat, tok), BF16),
            jax.ShapeDtypeStruct((exp_dev, units, width), BF16),
            jax.ShapeDtypeStruct((exp_dev, units, width), BF16),
        ),
        in_specs=[hbm] * 6,
        out_specs=(vmem, vmem, hbm, hbm),
        scratch_shapes=[
            pltpu.VMEM((feat, tok), BF16),
            pltpu.VMEM((1, tok), jnp.int32),
            pltpu.VMEM((1, tok), F32),
            pltpu.VMEM((feat, tok), BF16),
            pltpu.VMEM((slots, tok), BF16),
            rows, rows, rows, rows,
            pltpu.VMEM((2, CHUNKS, blocks, feat, length), BF16),
            pltpu.VMEM((2, CHUNKS, blocks, feat, length), BF16),
            pltpu.VMEM((2, CHUNKS, RING, 2, feat, half), BF16),
            pltpu.VMEM((2, CHUNKS, RING, 2, feat, length), BF16),
            pltpu.VMEM((2, CHUNKS, RING - 1, feat, length), BF16),
            weights, weights, turned_weights, turned_weights,
            pltpu.VMEM((exp_dev, units, slots // exp_dev), BF16),
            pltpu.VMEM((exp_dev, units, slots // exp_dev), BF16),
            weights, weights,
            dma((4,)),
            dma((2,)),
            dma((2, exp_dev)),
            dma((CHUNKS,)),
            dma((CHUNKS,)),
            dma((CHUNKS,)),
            dma((CHUNKS,)),
            dma((2, CHUNKS)),
            dma((2, CHUNKS, len(ARRIVALS))),
            dma((2, CHUNKS)),
            dma((2, CHUNKS, RING, 2)),
            dma((2, CHUNKS, RING, 2)),
            dma((2, CHUNKS, RING - 1)),
        ],
        compiler_params=pltpu.CompilerParams(
            collective_id=0, has_side_effects=True, vmem_limit_bytes=60 * 1024 * 1024
        ),
        name="expert_layer",
    )(tokens.T, routes.T, gate_value.T, weight_in.transpose(0, 2, 1), weight_out, cotangent.T)
    layer_out, grad_tokens, grad_in, grad_out = pl.pallas_call(
        hand_over,
        out_shape=tuple(jax.ShapeDtypeStruct(out.shape, out.dtype) for out in outs),
        in_specs=[hbm] * len(outs),
        out_specs=(hbm,) * len(outs),
        scratch_shapes=[pltpu.VMEM(out.shape, out.dtype) for out in outs] + [dma((2 + 2 * exp_dev,)), dma((2 + 2 * exp_dev,))],
        compiler_params=pltpu.CompilerParams(vmem_limit_bytes=60 * 1024 * 1024),
        name="hand_over",
    )(*outs)
    return layer_out.T, grad_tokens.T, grad_in.transpose(0, 2, 1), grad_out


def solution(mesh):
    in_specs = (
        P("expert", "hidden"),
        P("expert", None),
        P("expert", None),
        P("expert", None, "hidden"),
        P("expert", "hidden", None),
        P("expert", "hidden"),
    )
    out_specs = (
        P("expert", "hidden"),
        P("expert", "hidden"),
        P("expert", None, "hidden"),
        P("expert", "hidden", None),
    )
    return jax.shard_map(local, mesh=mesh, in_specs=in_specs, out_specs=out_specs, check_vma=False)
```
